256 devices in a mesh: gx: 16 (over z, core), gy: 16 (over x, y).
Axes of the slice: x: 4, y: 4, z: 8, core: 2. Of those that a mesh axis runs over, the one named last changes fastest.
Arguments:
- deflation: float32 [16, 16, 32, 16384], P('gx', 'gy'), may hold values from -0.1953125 to 0.1953125
- diag_stiff: float32 [16, 16, 16384], P('gx', 'gy'), may hold values from 3 to 12
- tile_vals: bfloat16 [16, 16, 128, 2, 128, 128], P('gx', 'gy'), may hold values from -1.25 to 1.25
- tile_cols: int32 [16, 16, 128, 2], P('gx', 'gy'), may hold values from 0 to 127
- west_coup: bfloat16 [16, 16, 32, 128, 128], P('gx', 'gy'), may hold values from -1.6970563 to 2.6970563
- north_coup: bfloat16 [16, 16, 32, 128, 128], P('gx', 'gy'), may hold values from -1.6970563 to 2.6970563
Outputs:
- coarse_blocks: float32 [16, 16, 3, 32, 32], P('gx', 'gy')
- pivots: float32 [16, 16, 32, 32], P('gx', 'gy')
- multipliers: float32 [16, 16, 32, 32], P('gx', 'gy')
The draws below stay inside these ranges and needn't reach their ends.
All inputs are finite; a program needn't handle non-finite values.
Results may differ from the reference program's by a relative error of at most 0.0003.
The reference program's roundings to bfloat16 on the way count: a program that leaves them out, or rounds other values in their place, can miss the bound.
Values sent between devices are 32-bit elements; how exact they have to be, the bound alone decides.
A program may use at most 64 MiB of HBM per device.

```python
import math
import jax
import jax.numpy as jnp
import numpy as np
from jax import lax

K = 32
TS = 128
NB = 2
FT = 32
NT = 128
NL = 16384
N_GX = 16
N_GY = 16


coupling_ratio = 0.501


stiff_mean = 9.0 / math.log(4.0)


mode_scales = (3.2, 1.8, 1.1, 0.65)


hadamard_rows = np.array([[1.0, 1.0, 1.0, 1.0], [1.0, -1.0, 1.0, -1.0], [1.0, 1.0, -1.0, -1.0], [1.0, -1.0, -1.0, 1.0]], np.float32)


def coupling_tiles(key):
    tile_shape = (N_GX, N_GY, FT, TS, TS)
    spread = 0.1 * math.sqrt(FT)
    offset_level = 4.0 * coupling_ratio * stiff_mean / TS
    values = jnp.clip(jax.random.normal(key, tile_shape, jnp.float32), -3.0, 3.0)
    return (offset_level + spread * values).astype(jnp.bfloat16)


def draw_west_coup(key, part):
    return coupling_tiles(jax.random.fold_in(key, 11))


def draw_north_coup(key, part):
    return coupling_tiles(jax.random.fold_in(key, 12))


def draw_diag_stiff(key, part):
    full_shape = (N_GX, N_GY, NL)
    local_key = jax.random.fold_in(key, 13)
    values = jnp.exp(jax.random.uniform(local_key, full_shape, jnp.float32, math.log(3.0), math.log(12.0)))
    return jnp.clip(values, 3.0, 12.0).astype(jnp.float32)


def draw_deflation(key, part):
    full_shape = (N_GX, N_GY, K, NL)
    mode_shape = (N_GX, N_GY, K, 4)
    rough_key = jax.random.fold_in(key, 21)
    mode_key = jax.random.fold_in(key, 22)
    rough_part = jnp.clip(jax.random.normal(rough_key, full_shape, jnp.float32), -4.0, 4.0)
    mode_coeffs = jnp.clip(jax.random.normal(mode_key, mode_shape, jnp.float32), -3.0, 3.0)
    tile_phase = jnp.arange(NT, dtype=jnp.int32) % 4
    patterns = jnp.asarray(hadamard_rows)[:, tile_phase]
    patterns = jnp.repeat(patterns, TS, axis=1)
    common_part = mode_scales[0] * mode_coeffs[..., 0:1] * patterns[0]
    common_part = common_part + mode_scales[1] * mode_coeffs[..., 1:2] * patterns[1]
    common_part = common_part + mode_scales[2] * mode_coeffs[..., 2:3] * patterns[2]
    common_part = common_part + mode_scales[3] * mode_coeffs[..., 3:4] * patterns[3]
    return ((rough_part + common_part) * (1.0 / math.sqrt(NL))).astype(jnp.float32)


def plant(drawn, own_key, least, high):
    dims = drawn.shape
    place = [jax.random.randint(jax.random.fold_in(own_key, axis), (), 0, dims[axis]) for axis in range(len(dims))]
    drawn = drawn.at[tuple(place)].set(least)
    longest = dims.index(max(dims))
    place[longest] = (place[longest] + 1) % dims[longest]
    return drawn.at[tuple(place)].set(high)


def shard_levels(own_key, dims, shards, smallest, top_value):
    def one(axis_at, blocks):
        steps = jax.random.uniform(jax.random.fold_in(jax.random.fold_in(own_key, 6), axis_at), (blocks,), jnp.float32, smallest / len(shards), top_value / len(shards))
        return jnp.repeat(jnp.exp(steps), dims[axis_at] // blocks).reshape((-1,) + (1,) * (len(dims) - axis_at - 1))

    level = one(*shards[0])
    for cut in shards[1:]:
        level = level * one(*cut)
    return level


def centred(own_key, extent, width, bound, cuts=(), held_as=jnp.bfloat16):
    values = jax.random.normal(own_key, extent, jnp.float32) * width
    if len(cuts) > 0:
        values = shard_levels(own_key, extent, cuts, -0.22, 0.18) * values
    return jnp.clip(values, min=-bound, max=bound).astype(held_as)


def setup_inputs(seed: int = 0) -> dict:
    streams_of = jax.random.split(jax.random.key(seed), 7)
    deflation = draw_deflation(jax.random.fold_in(streams_of[6], 71), 0)
    diag_stiff = draw_diag_stiff(jax.random.fold_in(streams_of[6], 71), 0)
    tile_vals = centred(streams_of[2], (N_GX, N_GY, NT, NB, TS, TS), (1600 * NB // NT) ** -0.5, 1.25, ((0, 16), (1, 16)))
    tile_cols = plant(jax.random.randint(streams_of[3], (N_GX, N_GY, NT, NB), 0, NT), jax.random.fold_in(streams_of[3], 1), 0, NT - 1).astype(jnp.int32)
    west_coup = draw_west_coup(jax.random.fold_in(streams_of[6], 71), 0)
    north_coup = draw_north_coup(jax.random.fold_in(streams_of[6], 71), 0)
    return dict(deflation=deflation, diag_stiff=diag_stiff, tile_vals=tile_vals, tile_cols=tile_cols, west_coup=west_coup, north_coup=north_coup)


HIGHEST = lax.Precision.HIGHEST

def to_bfloat(values):
    return lax.optimization_barrier(values.astype(jnp.bfloat16)).astype(jnp.float32)

def subdomain_self(inputs):
    vectors, weights, tile_block, column_ids = inputs
    count_vec, row_total = vectors.shape
    tile_size = tile_block.shape[-1]
    vector_tiles = vectors.reshape(count_vec, row_total // tile_size, tile_size)
    applied = jnp.einsum('krs,rjst->rjkt', to_bfloat(vector_tiles), tile_block.astype(jnp.float32), precision=HIGHEST)
    partners = vector_tiles[:, column_ids]
    cross_term = jnp.einsum('rjkt,lrjt->kl', applied, partners, precision=HIGHEST)
    gram_part = jnp.dot(vectors * weights[None, :], vectors.T, precision=HIGHEST)
    return gram_part + cross_term + cross_term.T

def schur_step(previous, diag_block, low_block):
    factor = jnp.linalg.cholesky(previous)
    solved = jax.scipy.linalg.cho_solve((factor, True), low_block.T)
    multiplier = solved.T
    pivot_block = diag_block - jnp.dot(multiplier, low_block.T, precision=HIGHEST)
    return (pivot_block, multiplier)

def line_factor(selfs, wests):

    def advance(previous, block_pair):
        pivot_block, multiplier = schur_step(previous, block_pair[0], block_pair[1])
        return (pivot_block, (pivot_block, multiplier))
    final_pivot, (pivot_rest, mult_rest) = lax.scan(advance, selfs[0], (selfs[1:], wests[1:]))
    pivots = jnp.concatenate([selfs[:1], pivot_rest], axis=0)
    multipliers = jnp.concatenate([jnp.zeros_like(wests[:1]), mult_rest], axis=0)
    return (pivots, multipliers)

def flatten_grid(values):
    return values.reshape((values.shape[0] * values.shape[1],) + values.shape[2:])

def reference(deflation, diag_stiff, tile_vals, tile_cols, west_coup, north_coup):
    grid_x, grid_y, count_vec, row_total = deflation.shape
    tile_size = tile_vals.shape[-1]
    band_tiles = west_coup.shape[2]
    self_blocks = lax.map(subdomain_self, (flatten_grid(deflation), flatten_grid(diag_stiff), flatten_grid(tile_vals), flatten_grid(tile_cols)))
    self_blocks = self_blocks.reshape(grid_x, grid_y, count_vec, count_vec)
    tiles_all = deflation.reshape(grid_x, grid_y, count_vec, row_total // tile_size, tile_size)
    west_round = to_bfloat(tiles_all[:, :, :, 0:band_tiles])
    north_round = to_bfloat(tiles_all[:, :, :, 2 * band_tiles:3 * band_tiles])
    west_proj = jnp.einsum('abkfs,abfst->abfkt', west_round, west_coup.astype(jnp.float32), precision=HIGHEST)
    north_proj = jnp.einsum('abkfs,abfst->abfkt', north_round, north_coup.astype(jnp.float32), precision=HIGHEST)
    east_band = tiles_all[:, :, :, band_tiles:2 * band_tiles]
    south_band = tiles_all[:, :, :, 3 * band_tiles:4 * band_tiles]
    from_west = jnp.concatenate([jnp.zeros_like(east_band[:, :1]), east_band[:, :-1]], axis=1)
    from_north = jnp.concatenate([jnp.zeros_like(south_band[:1]), south_band[:-1]], axis=0)
    west_block = -jnp.einsum('abfkt,ablft->abkl', west_proj, from_west, precision=HIGHEST)
    north_block = -jnp.einsum('abfkt,ablft->abkl', north_proj, from_north, precision=HIGHEST)
    coarse_blocks = jnp.stack([self_blocks, west_block, north_block], axis=2)
    pivots, multipliers = jax.vmap(line_factor)(self_blocks, west_block)
    return (coarse_blocks, pivots, multipliers)
```

```python
import functools

import jax
import jax.numpy as jnp
from jax import lax
from jax.experimental import pallas as pl
from jax.experimental.pallas import tpu as pltpu
from jax.sharding import PartitionSpec as P

MESH = pl.DeviceIdType.MESH
F32 = jnp.float32
BF16 = jnp.bfloat16
HIGHEST = lax.Precision.HIGHEST

K = 32
TS = 128
NT = 128
FT = 32
NL = NT * TS
ROW = 16
COL = 16
HALF = 16
WIDE = HALF * TS
CHUNKS = 16
PER = NT // CHUNKS
NT_DIMS = (((1,), (1,)), ((), ()))


def halves(values):
    high = values.astype(BF16)
    low = (values - high.astype(F32)).astype(BF16)
    return high, low


def stacked(values):
    high, low = halves(values)
    return jnp.concatenate([high, low], axis=0)


def folded(total):
    return (
        total[0:K, 0:K] + total[0:K, K : 2 * K] + total[K : 2 * K, 0:K] + total[K : 2 * K, K : 2 * K]
    )


def nt_dot(left, right):
    return lax.dot_general(left, right, NT_DIMS, preferred_element_type=F32)


def blocks_kernel(
    defl_hbm, diag_ref, vals_hbm, cols_ref, west_hbm, north_hbm,
    out_ref,
    vec, pair, vals, west, north, proj_w, proj_n,
    got_e, got_s, got_pw, got_pn, mine, slots, got_n, sent_n,
    sem_in, sem_vals, send_band, recv_band, send_row, recv_row, send_n, recv_n,
):
    row = lax.axis_index("gx")
    col = lax.axis_index("gy")
    east = {"gy": lax.rem(col + 1, COL)}
    west_of = {"gy": lax.rem(col + COL - 1, COL)}
    south = {"gx": lax.rem(row + 1, ROW)}
    north_of = {"gx": lax.rem(row + ROW - 1, ROW)}

    load_vec = pltpu.make_async_copy(defl_hbm.at[0, 0], vec, sem_in.at[0])
    load_west = pltpu.make_async_copy(west_hbm.at[0, 0], west, sem_in.at[1])
    load_north = pltpu.make_async_copy(north_hbm.at[0, 0], north, sem_in.at[2])
    load_vec.start()
    load_west.start()
    load_north.start()
    load_vals = []
    for c in range(CHUNKS):
        part = pl.ds(c * PER, PER)
        load_vals.append(
            pltpu.make_async_copy(vals_hbm.at[0, 0, part], vals.at[part], sem_vals.at[c])
        )
        load_vals[-1].start()

    barrier = pltpu.get_barrier_semaphore()
    for step in range(1, COL):
        pl.semaphore_signal(
            barrier, inc=1, device_id={"gy": lax.rem(col + step, COL)}, device_id_type=MESH
        )
    pl.semaphore_signal(barrier, inc=1, device_id=south, device_id_type=MESH)
    pl.semaphore_signal(barrier, inc=1, device_id=north_of, device_id_type=MESH)
    pl.semaphore_wait(barrier, COL + 1)

    def remote(source, target, at, device):
        copy = pltpu.make_async_remote_copy(
            src_ref=source,
            dst_ref=target,
            send_sem=send_band.at[at],
            recv_sem=recv_band.at[at],
            device_id=device,
            device_id_type=MESH,
        )
        copy.start()
        return copy

    move_e = remote(defl_hbm.at[0, 0, :, pl.ds(FT * TS, WIDE)], got_e, 0, east)
    move_s = remote(defl_hbm.at[0, 0, :, pl.ds(3 * FT * TS, WIDE)], got_s, 1, south)

    load_vec.wait()

    def split(c, total):
        part = pl.ds(pl.multiple_of(c * 1024, 1024), 1024)
        values = vec[:, part]
        both = stacked(values)
        for t in range(8):
            pair[c * 8 + t] = both[:, t * TS : (t + 1) * TS]
        scaled = stacked(values * (diag_ref[0, :, part] * 0.5))
        return total + nt_dot(scaled, both)

    total = lax.fori_loop(0, NL // 1024, split, jnp.zeros((2 * K, 2 * K), F32))

    def project(tiles, first, target):
        def one(f, carry):
            place = pl.ds(pl.multiple_of(f * TS, TS), TS)
            target[:, place] = jnp.dot(
                pair[first + f, 0:K], tiles[f], preferred_element_type=F32
            )
            return carry

        return one

    load_west.wait()
    lax.fori_loop(HALF, FT, project(west, 0, proj_w), 0, unroll=4)
    move_pw = remote(proj_w.at[:, pl.ds(WIDE, FT * TS - WIDE)], got_pw, 2, west_of)
    load_north.wait()
    lax.fori_loop(HALF, FT, project(north, 2 * FT, proj_n), 0, unroll=4)
    move_pn = remote(proj_n.at[:, pl.ds(WIDE, FT * TS - WIDE)], got_pn, 3, north_of)
    lax.fori_loop(0, HALF, project(west, 0, proj_w), 0, unroll=4)
    lax.fori_loop(0, HALF, project(north, 2 * FT, proj_n), 0, unroll=4)

    def tile_row(r, total):
        own = pair[r, 0:K]
        left, right = [], []
        for j in range(2):
            left.append(stacked(jnp.dot(own, vals[r, j], preferred_element_type=F32)))
            right.append(pair[cols_ref[0, 0, r, j]])
        return total + nt_dot(jnp.concatenate(left, axis=1), jnp.concatenate(right, axis=1))

    for c in range(CHUNKS):
        load_vals[c].wait()
        total = lax.fori_loop(c * PER, (c + 1) * PER, tile_row, total, unroll=8)
    cross = folded(total)
    self_block = cross + cross.T

    def band(left, left_at, right, right_at, count):
        def one(c, acc):
            a = left[:, pl.ds(pl.multiple_of(left_at + c * 512, 512), 512)]
            b = right[:, pl.ds(pl.multiple_of(right_at + c * 512, 512), 512)]
            return acc + nt_dot(stacked(a), stacked(b))

        return -folded(lax.fori_loop(0, count // 512, one, jnp.zeros((2 * K, 2 * K), F32)))

    move_e.wait_recv()
    west_here = jnp.where(col > 0, band(proj_w, 0, got_e, 0, WIDE), 0.0)
    move_pw.wait_recv()
    west_next = band(got_pw, 0, vec, FT * TS + WIDE, FT * TS - WIDE)
    move_pn.wait_recv()
    sent_n[:, 0:K] = band(got_pn, 0, vec, 3 * FT * TS + WIDE, FT * TS - WIDE)
    move_n = pltpu.make_async_remote_copy(
        src_ref=sent_n, dst_ref=got_n, send_sem=send_n, recv_sem=recv_n,
        device_id=south, device_id_type=MESH,
    )
    move_n.start()
    mine[...] = jnp.concatenate([self_block, west_here, west_next, west_next], axis=1)

    def to_row(step):
        return pltpu.make_async_remote_copy(
            src_ref=mine,
            dst_ref=slots.at[step - 1],
            send_sem=send_row.at[step - 1],
            recv_sem=recv_row.at[step - 1],
            device_id={"gy": lax.rem(col + step, COL)},
            device_id_type=MESH,
        )

    for step in range(1, COL):
        @pl.when(col + step < COL)
        def _():
            to_row(step).start()

    move_s.wait_recv()
    north_here = band(proj_n, 0, got_s, 0, WIDE)
    move_n.wait_recv()
    north_block = jnp.where(row > 0, north_here + got_n[:, 0:K], 0.0)
    out_ref[COL - 1] = jnp.concatenate(
        [self_block, west_here, west_next, north_block], axis=1
    )

    for step in range(1, COL):
        @pl.when(col >= step)
        def _():
            to_row(step).wait_recv()
            out_ref[step - 1] = slots[step - 1]

        @pl.when(col < step)
        def _():
            out_ref[step - 1] = jnp.zeros((K, 4 * K), F32)

        @pl.when(col + step < COL)
        def _():
            to_row(step).wait_send()

    move_e.wait_send()
    move_s.wait_send()
    move_pw.wait_send()
    move_pn.wait_send()
    move_n.wait_send()


def made_blocks(defl, diag, vals, cols, west, north):
    hbm = pl.BlockSpec(memory_space=pl.ANY)
    vmem = pl.BlockSpec(memory_space=pltpu.VMEM)
    return pl.pallas_call(
        blocks_kernel,
        out_shape=jax.ShapeDtypeStruct((COL, K, 4 * K), F32),
        in_specs=[hbm, vmem, hbm, pl.BlockSpec(memory_space=pltpu.SMEM), hbm, hbm],
        out_specs=vmem,
        scratch_shapes=[
            pltpu.VMEM((K, NL), F32),
            pltpu.VMEM((NT, 2 * K, TS), BF16),
            pltpu.VMEM((NT, 2, TS, TS), BF16),
            pltpu.VMEM((FT, TS, TS), BF16),
            pltpu.VMEM((FT, TS, TS), BF16),
            pltpu.VMEM((K, FT * TS), F32),
            pltpu.VMEM((K, FT * TS), F32),
            pltpu.VMEM((K, WIDE), F32),
            pltpu.VMEM((K, WIDE), F32),
            pltpu.VMEM((K, FT * TS - WIDE), F32),
            pltpu.VMEM((K, FT * TS - WIDE), F32),
            pltpu.VMEM((K, 4 * K), F32),
            pltpu.VMEM((COL - 1, K, 4 * K), F32),
            pltpu.VMEM((K, 4 * K), F32),
            pltpu.VMEM((K, 4 * K), F32),
            pltpu.SemaphoreType.DMA((3,)),
            pltpu.SemaphoreType.DMA((CHUNKS,)),
            pltpu.SemaphoreType.DMA((4,)),
            pltpu.SemaphoreType.DMA((4,)),
            pltpu.SemaphoreType.DMA((COL - 1,)),
            pltpu.SemaphoreType.DMA((COL - 1,)),
            pltpu.SemaphoreType.DMA,
            pltpu.SemaphoreType.DMA,
        ],
        compiler_params=pltpu.CompilerParams(
            collective_id=0, has_side_effects=True, vmem_limit_bytes=48 * 2**20
        ),
    )(defl, diag, vals, cols, west, north)


def exact(left, right):
    return jnp.dot(left, right, precision=HIGHEST, preferred_element_type=F32)


def exact_nt(left, right):
    return lax.dot_general(left, right, NT_DIMS, precision=HIGHEST, preferred_element_type=F32)


PANEL = 8


def inverse(packs):
    shape = (K, 4 * K)
    lane = lax.broadcasted_iota(jnp.int32, shape, 1)
    sub = lax.broadcasted_iota(jnp.int32, shape, 0)
    base = lane - lax.rem(lane, K)
    within = lax.rem(lane, K)
    packs = list(packs)
    for first in range(0, K, PANEL):
        panels = [
            [jnp.take_along_axis(m, base + (first + q), axis=1) for q in range(PANEL)]
            for m in packs
        ]
        for q in range(PANEL):
            k = first + q
            is_row = sub == k
            is_lane = within == k
            for at, m in enumerate(packs):
                panel = panels[at]
                column = panel[q]
                scale = 1.0 / column[k : k + 1]
                for later in range(q + 1, PANEL):
                    part = panel[later][k : k + 1] * scale
                    panel[later] = jnp.where(is_row, part, panel[later] - column * part)
                line = jnp.where(is_lane[0:1], 1.0, m[k : k + 1]) * scale
                packs[at] = jnp.where(is_row, line, jnp.where(is_lane, 0.0, m) - column * line)
    return packs


def chain_kernel(got_ref, coarse_ref, pivot_ref, mult_ref):
    col = lax.axis_index("gy")
    own = got_ref[COL - 1]
    self_own = own[:, 0:K]
    north_own = own[:, 3 * K : 4 * K]
    eye = (
        lax.broadcasted_iota(jnp.int32, (K, K), 0) == lax.broadcasted_iota(jnp.int32, (K, K), 1)
    ).astype(F32)
    nodes = {}
    links = {}
    for k in range(COL - 1):
        nodes[k] = jnp.where(k < col, got_ref[k][:, 0:K], eye)
    for k in range(COL - 2):
        link = got_ref[k][:, K : 2 * K] + got_ref[k + 1][:, 2 * K : 3 * K]
        link = jnp.where(k < col, link, 0.0)
        links[k] = (link, link.T)
    west_own = own[:, K : 2 * K] + got_ref[0][:, 2 * K : 3 * K]
    west_own = jnp.where(col > 0, west_own, 0.0)

    stride = 1
    while stride < COL - 1:
        gone = list(range(stride, COL - 1, 2 * stride))
        padded = gone + [gone[-1]] * (-len(gone) % 4)
        packs = [
            jnp.concatenate([nodes[k] for k in padded[at : at + 4]], axis=1)
            for at in range(0, len(padded), 4)
        ]
        packs = inverse(packs)
        fresh = {}
        for at, k in enumerate(gone):
            inv = packs[at // 4][:, (at % 4) * K : (at % 4 + 1) * K]
            near, near_t = links[k - stride]
            if k + stride < COL - 1:
                far, far_t = links[k]
                outer = exact(jnp.concatenate([near, far_t], axis=0), inv)
                to_near = exact_nt(outer, near)
                to_far = exact(outer, far)
                nodes[k - stride] = nodes[k - stride] - to_near[0:K]
                nodes[k + stride] = nodes[k + stride] - to_far[K : 2 * K]
                fresh[k - stride] = (-to_far[0:K], -to_near[K : 2 * K])
            else:
                nodes[k - stride] = nodes[k - stride] - exact_nt(exact(near, inv), near)
        links = fresh
        stride *= 2
    [pack] = inverse([jnp.concatenate([nodes[0]] * 4, axis=1)])
    mult = exact(west_own, pack[:, 0:K])
    pivot_ref[0, 0] = self_own - exact_nt(mult, west_own)
    mult_ref[0, 0] = mult
    coarse_ref[0, 0, 0] = self_own
    coarse_ref[0, 0, 1] = west_own
    coarse_ref[0, 0, 2] = north_own


def local(defl, diag, vals, cols, west, north):
    got = made_blocks(defl, diag, vals, cols, west, north)
    vmem = pl.BlockSpec(memory_space=pltpu.VMEM)
    return pl.pallas_call(
        chain_kernel,
        out_shape=(
            jax.ShapeDtypeStruct((1, 1, 3, K, K), F32),
            jax.ShapeDtypeStruct((1, 1, K, K), F32),
            jax.ShapeDtypeStruct((1, 1, K, K), F32),
        ),
        in_specs=[vmem],
        out_specs=(vmem, vmem, vmem),
        compiler_params=pltpu.CompilerParams(vmem_limit_bytes=16 * 2**20),
    )(got)


def solution(mesh):
    placed = (
        P("gx", "gy", None, None),
        P("gx", "gy", None),
        P("gx", "gy", None, None, None, None),
        P("gx", "gy", None, None),
        P("gx", "gy", None, None, None),
        P("gx", "gy", None, None, None),
    )
    return jax.shard_map(
        local,
        mesh=mesh,
        in_specs=placed,
        out_specs=(
            P("gx", "gy", None, None, None),
            P("gx", "gy", None, None),
            P("gx", "gy", None, None),
        ),
        check_vma=False,
    )
```

```python
import functools

import jax
import jax.numpy as jnp
from jax import lax
from jax.experimental import pallas as pl
from jax.experimental.pallas import tpu as pltpu
from jax.sharding import PartitionSpec as P

MESH = pl.DeviceIdType.MESH
F32 = jnp.float32
BF16 = jnp.bfloat16
HIGHEST = lax.Precision.HIGHEST

K = 32
TS = 128
NT = 128
FT = 32
NL = NT * TS
ROW = 16
COL = 16
HALF = 16
WIDE = HALF * TS
CHUNKS = 8
PER = NT // CHUNKS
NT_DIMS = (((1,), (1,)), ((), ()))


def halves(values):
    high = values.astype(BF16)
    low = (values - high.astype(F32)).astype(BF16)
    return high, low


def stacked(values):
    high, low = halves(values)
    return jnp.concatenate([high, low], axis=0)


def folded(total):
    return (
        total[0:K, 0:K] + total[0:K, K : 2 * K] + total[K : 2 * K, 0:K] + total[K : 2 * K, K : 2 * K]
    )


def nt_dot(left, right):
    return lax.dot_general(left, right, NT_DIMS, preferred_element_type=F32)


def blocks_kernel(
    defl_hbm, diag_ref, vals_hbm, cols_ref, west_hbm, north_hbm,
    out_ref,
    vec, pair, vals, west, north, proj_w, proj_n,
    got_e, got_s, got_pw, got_pn, mine, slots, got_n, sent_n,
    sem_in, sem_vals, send_band, recv_band, send_row, recv_row, send_n, recv_n,
):
    row = lax.axis_index("gx")
    col = lax.axis_index("gy")
    east = {"gy": lax.rem(col + 1, COL)}
    west_of = {"gy": lax.rem(col + COL - 1, COL)}
    south = {"gx": lax.rem(row + 1, ROW)}
    north_of = {"gx": lax.rem(row + ROW - 1, ROW)}

    load_vec = pltpu.make_async_copy(defl_hbm.at[0, 0], vec, sem_in.at[0])
    load_west = pltpu.make_async_copy(west_hbm.at[0, 0], west, sem_in.at[1])
    load_north = pltpu.make_async_copy(north_hbm.at[0, 0], north, sem_in.at[2])
    load_vec.start()
    load_west.start()
    load_north.start()

    def load_vals(c):
        part = pl.ds(c * PER, PER)
        return pltpu.make_async_copy(vals_hbm.at[0, 0, part], vals.at[part], sem_vals.at[c])

    for c in range(CHUNKS):
        load_vals(c).start()

    barrier = pltpu.get_barrier_semaphore()
    def greet(there, device):
        @pl.when(there)
        def _():
            pl.semaphore_signal(barrier, inc=1, device_id=device, device_id_type=MESH)

    for step in range(1, COL):
        greet(col >= step, {"gy": lax.rem(col + COL - step, COL)})
    greet(col < COL - 1, east)
    greet(row < ROW - 1, south)
    greet(row > 0, north_of)
    partners = (
        (COL - 1 - col)
        + jnp.where(col > 0, 1, 0)
        + jnp.where(row < ROW - 1, 1, 0)
        + jnp.where(row > 0, 1, 0)
    )
    pl.semaphore_wait(barrier, partners)

    def remote(source, target, at, device):
        return pltpu.make_async_remote_copy(
            src_ref=source,
            dst_ref=target,
            send_sem=send_band.at[at],
            recv_sem=recv_band.at[at],
            device_id=device,
            device_id_type=MESH,
        )

    move_e = remote(defl_hbm.at[0, 0, :, pl.ds(FT * TS, WIDE)], got_e, 0, east)
    move_s = remote(defl_hbm.at[0, 0, :, pl.ds(3 * FT * TS, WIDE)], got_s, 1, south)
    move_pw = remote(proj_w.at[:, pl.ds(WIDE, FT * TS - WIDE)], got_pw, 2, west_of)
    move_pn = remote(proj_n.at[:, pl.ds(WIDE, FT * TS - WIDE)], got_pn, 3, north_of)
    pl.when(col < COL - 1)(move_e.start)
    pl.when(row < ROW - 1)(move_s.start)

    load_vec.wait()

    def split(c, total):
        part = pl.ds(pl.multiple_of(c * 1024, 1024), 1024)
        values = vec[:, part]
        both = stacked(values)
        for t in range(8):
            pair[c * 8 + t] = both[:, t * TS : (t + 1) * TS]
        scaled = stacked(values * (diag_ref[0, :, part] * 0.5))
        return total + nt_dot(scaled, both)

    total = lax.fori_loop(0, NL // 1024, split, jnp.zeros((2 * K, 2 * K), F32), unroll=4)

    def project(tiles, first, target):
        def one(f, carry):
            place = pl.ds(pl.multiple_of(f * TS, TS), TS)
            target[:, place] = jnp.dot(
                pair[first + f, 0:K], tiles[f], preferred_element_type=F32
            )
            return carry

        return one

    load_west.wait()
    lax.fori_loop(HALF, FT, project(west, 0, proj_w), 0, unroll=4)
    pl.when(col > 0)(move_pw.start)
    load_north.wait()
    lax.fori_loop(HALF, FT, project(north, 2 * FT, proj_n), 0, unroll=4)
    pl.when(row > 0)(move_pn.start)
    lax.fori_loop(0, HALF, project(west, 0, proj_w), 0, unroll=4)
    lax.fori_loop(0, HALF, project(north, 2 * FT, proj_n), 0, unroll=4)

    def tile_rows(c, total):
        load_vals(c).wait()
        for i in range(PER):
            r = c * PER + i
            tiles = jnp.concatenate([vals[r, 0], vals[r, 1]], axis=1)
            left = jnp.dot(pair[r, 0:K], tiles, preferred_element_type=F32)
            right = jnp.concatenate([pair[cols_ref[0, 0, j, r]] for j in range(2)], axis=1)
            total = total + nt_dot(stacked(left), right)
        return total

    total = lax.fori_loop(0, CHUNKS, tile_rows, total)
    cross = folded(total)
    self_block = cross + cross.T

    def band(left, left_at, right, right_at, count):
        def one(c, acc):
            a = left[:, pl.ds(pl.multiple_of(left_at + c * 512, 512), 512)]
            b = right[:, pl.ds(pl.multiple_of(right_at + c * 512, 512), 512)]
            return acc + nt_dot(stacked(a), stacked(b))

        return -folded(lax.fori_loop(0, count // 512, one, jnp.zeros((2 * K, 2 * K), F32)))

    pl.when(col > 0)(move_e.wait_recv)
    west_here = jnp.where(col > 0, band(proj_w, 0, got_e, 0, WIDE), 0.0)
    pl.when(col < COL - 1)(move_pw.wait_recv)
    west_next = band(got_pw, 0, vec, FT * TS + WIDE, FT * TS - WIDE)
    pl.when(row < ROW - 1)(move_pn.wait_recv)
    sent_n[:, 0:K] = band(got_pn, 0, vec, 3 * FT * TS + WIDE, FT * TS - WIDE)
    move_n = pltpu.make_async_remote_copy(
        src_ref=sent_n, dst_ref=got_n, send_sem=send_n, recv_sem=recv_n,
        device_id=south, device_id_type=MESH,
    )
    pl.when(row < ROW - 1)(move_n.start)
    mine[...] = jnp.concatenate([self_block, west_here, west_next, west_next], axis=1)

    def to_row(step):
        return pltpu.make_async_remote_copy(
            src_ref=mine,
            dst_ref=slots.at[step - 1],
            send_sem=send_row.at[step - 1],
            recv_sem=recv_row.at[step - 1],
            device_id={"gy": lax.rem(col + step, COL)},
            device_id_type=MESH,
        )

    for step in range(1, COL):
        @pl.when(col + step < COL)
        def _():
            to_row(step).start()

    pl.when(row > 0)(move_s.wait_recv)
    north_here = band(proj_n, 0, got_s, 0, WIDE)
    pl.when(row > 0)(move_n.wait_recv)
    north_block = jnp.where(row > 0, north_here + got_n[:, 0:K], 0.0)
    out_ref[COL - 1] = jnp.concatenate(
        [self_block, west_here, west_next, north_block], axis=1
    )

    for step in range(1, COL):
        @pl.when(col >= step)
        def _():
            to_row(step).wait_recv()
            out_ref[step - 1] = slots[step - 1]

        @pl.when(col < step)
        def _():
            out_ref[step - 1] = jnp.zeros((K, 4 * K), F32)

        @pl.when(col + step < COL)
        def _():
            to_row(step).wait_send()

    pl.when(col < COL - 1)(move_e.wait_send)
    pl.when(row < ROW - 1)(move_s.wait_send)
    pl.when(col > 0)(move_pw.wait_send)
    pl.when(row > 0)(move_pn.wait_send)
    pl.when(row < ROW - 1)(move_n.wait_send)


def made_blocks(defl, diag, vals, cols, west, north):
    hbm = pl.BlockSpec(memory_space=pl.ANY)
    vmem = pl.BlockSpec(memory_space=pltpu.VMEM)
    return pl.pallas_call(
        blocks_kernel,
        out_shape=jax.ShapeDtypeStruct((COL, K, 4 * K), F32),
        in_specs=[hbm, vmem, hbm, pl.BlockSpec(memory_space=pltpu.SMEM), hbm, hbm],
        out_specs=vmem,
        scratch_shapes=[
            pltpu.VMEM((K, NL), F32),
            pltpu.VMEM((NT, 2 * K, TS), BF16),
            pltpu.VMEM((NT, 2, TS, TS), BF16),
            pltpu.VMEM((FT, TS, TS), BF16),
            pltpu.VMEM((FT, TS, TS), BF16),
            pltpu.VMEM((K, FT * TS), F32),
            pltpu.VMEM((K, FT * TS), F32),
            pltpu.VMEM((K, WIDE), F32),
            pltpu.VMEM((K, WIDE), F32),
            pltpu.VMEM((K, FT * TS - WIDE), F32),
            pltpu.VMEM((K, FT * TS - WIDE), F32),
            pltpu.VMEM((K, 4 * K), F32),
            pltpu.VMEM((COL - 1, K, 4 * K), F32),
            pltpu.VMEM((K, 4 * K), F32),
            pltpu.VMEM((K, 4 * K), F32),
            pltpu.SemaphoreType.DMA((3,)),
            pltpu.SemaphoreType.DMA((CHUNKS,)),
            pltpu.SemaphoreType.DMA((4,)),
            pltpu.SemaphoreType.DMA((4,)),
            pltpu.SemaphoreType.DMA((COL - 1,)),
            pltpu.SemaphoreType.DMA((COL - 1,)),
            pltpu.SemaphoreType.DMA,
            pltpu.SemaphoreType.DMA,
        ],
        compiler_params=pltpu.CompilerParams(
            collective_id=0, has_side_effects=True, vmem_limit_bytes=60 * 2**20
        ),
    )(defl, diag, vals, cols, west, north)


def exact(left, right):
    return jnp.dot(left, right, precision=HIGHEST, preferred_element_type=F32)


def exact_nt(left, right):
    return lax.dot_general(left, right, NT_DIMS, precision=HIGHEST, preferred_element_type=F32)


def inverse(packs, width):
    shape = (K, 4 * K)
    lane = lax.broadcasted_iota(jnp.int32, shape, 1)
    sub = lax.broadcasted_iota(jnp.int32, shape, 0)
    within = lax.rem(lane, K)
    base = lane - within
    packs = list(packs)
    for first in range(0, K, width):
        panels = [
            [jnp.take_along_axis(m, base + (first + q), axis=1) for q in range(width)]
            for m in packs
        ]
        for q in range(width):
            k = first + q
            is_row = sub == k
            is_lane = within == k
            for at, m in enumerate(packs):
                panel = panels[at]
                column = panel[q]
                scale = 1.0 / column[k : k + 1]
                for later in range(q + 1, width):
                    part = panel[later][k : k + 1] * scale
                    panel[later] = jnp.where(is_row, part, panel[later] - column * part)
                line = jnp.where(is_lane[0:1], 1.0, m[k : k + 1]) * scale
                packs[at] = jnp.where(is_row, line, jnp.where(is_lane, 0.0, m) - column * line)
    return packs


NODES = COL - 1


def chain_kernel(got_ref, coarse_ref, pivot_ref, mult_ref, nodes, links, turned):
    col = lax.axis_index("gy")
    own = got_ref[COL - 1]
    self_own = own[:, 0:K]
    west_own = own[:, K : 2 * K] + got_ref[0][:, 2 * K : 3 * K]
    west_own = jnp.where(col > 0, west_own, 0.0)
    coarse_ref[0, 0, 0] = self_own
    coarse_ref[0, 0, 1] = west_own
    coarse_ref[0, 0, 2] = own[:, 3 * K : 4 * K]
    eye = (
        lax.broadcasted_iota(jnp.int32, (K, K), 0) == lax.broadcasted_iota(jnp.int32, (K, K), 1)
    ).astype(F32)
    nodes[0] = jnp.where(col > 0, got_ref[0][:, 0:K], eye)

    def level(stride):
        if stride == 1:
            held, fresh_links = {}, {}
            for k in range(NODES):
                held[k] = jnp.where(k < col, got_ref[k][:, 0:K], eye)
            for k in range(NODES - 1):
                link = got_ref[k][:, K : 2 * K] + got_ref[k + 1][:, 2 * K : 3 * K]
                link = jnp.where(k < col, link, 0.0)
                fresh_links[k] = (link, link.T)
        else:
            held = {k: nodes[k] for k in range(0, NODES, stride)}
            fresh_links = {k: (links[k], turned[k]) for k in range(0, NODES - stride, stride)}
        gone = list(range(stride, NODES, 2 * stride))
        if len(gone) == 1:
            packs = [jnp.concatenate([held[gone[0]]] * 4, axis=1)]
        else:
            padded = gone + [gone[-1]] * (-len(gone) % 4)
            packs = [
                jnp.concatenate([held[k] for k in padded[at : at + 4]], axis=1)
                for at in range(0, len(padded), 4)
            ]
        packs = inverse(packs, 8 if len(packs) > 1 else 16)
        for at, k in enumerate(gone):
            inv = packs[at // 4][:, (at % 4) * K : (at % 4 + 1) * K]
            near, near_t = fresh_links[k - stride]
            if k + stride < NODES:
                far, far_t = fresh_links[k]
                outer = exact(jnp.concatenate([near, far_t], axis=0), inv)
                to_near = exact_nt(outer, near)
                to_far = exact(outer, far)
                held[k - stride] = held[k - stride] - to_near[0:K]
                held[k + stride] = held[k + stride] - to_far[K : 2 * K]
                links[k - stride] = -to_far[0:K]
                turned[k - stride] = -to_near[K : 2 * K]
            else:
                held[k - stride] = held[k - stride] - exact_nt(exact(near, inv), near)
        for k in range(0, NODES, 2 * stride):
            nodes[k] = held[k]

    for stride in (1, 2, 4, 8):
        pl.when(col > stride)(functools.partial(level, stride))
    [pack] = inverse([jnp.concatenate([nodes[0]] * 4, axis=1)], 16)
    mult = exact(west_own, pack[:, 0:K])
    pivot_ref[0, 0] = self_own - exact_nt(mult, west_own)
    mult_ref[0, 0] = mult


def local(defl, diag, vals, cols, west, north):
    got = made_blocks(defl, diag, vals, jnp.swapaxes(cols, 2, 3), west, north)
    vmem = pl.BlockSpec(memory_space=pltpu.VMEM)
    return pl.pallas_call(
        chain_kernel,
        out_shape=(
            jax.ShapeDtypeStruct((1, 1, 3, K, K), F32),
            jax.ShapeDtypeStruct((1, 1, K, K), F32),
            jax.ShapeDtypeStruct((1, 1, K, K), F32),
        ),
        in_specs=[vmem],
        out_specs=(vmem, vmem, vmem),
        scratch_shapes=[pltpu.VMEM((NODES, K, K), F32)] * 3,
        compiler_params=pltpu.CompilerParams(vmem_limit_bytes=16 * 2**20),
    )(got)


def solution(mesh):
    placed = (
        P("gx", "gy", None, None),
        P("gx", "gy", None),
        P("gx", "gy", None, None, None, None),
        P("gx", "gy", None, None),
        P("gx", "gy", None, None, None),
        P("gx", "gy", None, None, None),
    )
    return jax.shard_map(
        local,
        mesh=mesh,
        in_specs=placed,
        out_specs=(
            P("gx", "gy", None, None, None),
            P("gx", "gy", None, None),
            P("gx", "gy", None, None),
        ),
        check_vma=False,
    )
```

```python
import functools

import jax
import jax.numpy as jnp
from jax import lax
from jax.experimental import pallas as pl
from jax.experimental.pallas import tpu as pltpu
from jax.sharding import PartitionSpec as P

MESH = pl.DeviceIdType.MESH
F32 = jnp.float32
BF16 = jnp.bfloat16
HIGHEST = lax.Precision.HIGHEST

K = 32
TS = 128
NT = 128
FT = 32
NL = NT * TS
ROW = 16
COL = 16
HALF = 16
WIDE = HALF * TS
CHUNKS = 8
PER = NT // CHUNKS
NT_DIMS = (((1,), (1,)), ((), ()))


def halves(values):
    high = values.astype(BF16)
    low = (values - high.astype(F32)).astype(BF16)
    return high, low


def stacked(values):
    high, low = halves(values)
    return jnp.concatenate([high, low], axis=0)


def folded(total):
    return (
        total[0:K, 0:K] + total[0:K, K : 2 * K] + total[K : 2 * K, 0:K] + total[K : 2 * K, K : 2 * K]
    )


def nt_dot(left, right):
    return lax.dot_general(left, right, NT_DIMS, preferred_element_type=F32)


def exact(left, right):
    return jnp.dot(left, right, precision=HIGHEST, preferred_element_type=F32)


def exact_nt(left, right):
    return lax.dot_general(left, right, NT_DIMS, precision=HIGHEST, preferred_element_type=F32)


def inverses(blocks, width):
    lane = lax.broadcasted_iota(jnp.int32, (K, K), 1)
    sub = lax.broadcasted_iota(jnp.int32, (K, K), 0)
    blocks = list(blocks)
    for first in range(0, K, width):
        panels = [
            [jnp.broadcast_to(m[:, first + q : first + q + 1], (K, K)) for q in range(width)]
            for m in blocks
        ]
        for q in range(width):
            k = first + q
            is_row = sub == k
            is_lane = lane == k
            for at, m in enumerate(blocks):
                panel = panels[at]
                column = panel[q]
                scale = 1.0 / column[k : k + 1]
                for later in range(q + 1, width):
                    part = panel[later][k : k + 1] * scale
                    panel[later] = jnp.where(is_row, part, panel[later] - column * part)
                line = jnp.where(is_lane[0:1], 1.0, m[k : k + 1]) * scale
                blocks[at] = jnp.where(is_row, line, jnp.where(is_lane, 0.0, m) - column * line)
    return blocks


def blocks_kernel(
    defl_hbm, diag_ref, vals_hbm, cols_ref, west_hbm, north_hbm,
    out_ref,
    vec, pair, vals, west, north, here_w, here_n, proj_w, proj_n,
    got_e, got_s, got_pw, got_pn, mine, slots, got_n, sent_n,
    sem_in, sem_vals, send_band, recv_band, send_row, recv_row, send_n, recv_n,
):
    row = lax.axis_index("gx")
    col = lax.axis_index("gy")
    east = {"gy": lax.rem(col + 1, COL)}
    west_of = {"gy": lax.rem(col + COL - 1, COL)}
    south = {"gx": lax.rem(row + 1, ROW)}
    north_of = {"gx": lax.rem(row + ROW - 1, ROW)}

    load_vec = pltpu.make_async_copy(defl_hbm.at[0, 0], vec, sem_in.at[0])
    load_west = pltpu.make_async_copy(west_hbm.at[0, 0], west, sem_in.at[1])
    load_north = pltpu.make_async_copy(north_hbm.at[0, 0], north, sem_in.at[2])
    load_vec.start()
    load_west.start()
    load_north.start()

    barrier = pltpu.get_barrier_semaphore()

    def greet(there, device):
        @pl.when(there)
        def _():
            pl.semaphore_signal(barrier, inc=1, device_id=device, device_id_type=MESH)

    for step in range(1, COL):
        greet(col >= step, {"gy": lax.rem(col + COL - step, COL)})
    greet(col < COL - 1, east)
    greet(row < ROW - 1, south)
    greet(row > 0, north_of)
    partners = (
        (COL - 1 - col)
        + jnp.where(col > 0, 1, 0)
        + jnp.where(row < ROW - 1, 1, 0)
        + jnp.where(row > 0, 1, 0)
    )

    def load_vals(c):
        part = pl.ds(c * PER, PER)
        return pltpu.make_async_copy(vals_hbm.at[0, 0, part], vals.at[part], sem_vals.at[c])

    load_vec.wait()
    for c in range(CHUNKS):
        load_vals(c).start()

    def split(c, total):
        part = pl.ds(pl.multiple_of(c * 1024, 1024), 1024)
        values = vec[:, part]
        both = stacked(values)
        for t in range(8):
            pair[c * 8 + t] = both[:, t * TS : (t + 1) * TS]
        scaled = stacked(values * (diag_ref[0, :, part] * 0.5))
        return total + nt_dot(scaled, both)

    def project(tiles, first, f):
        return jnp.dot(pair[first + f, 0:K], tiles[f], preferred_element_type=F32)

    def send_off(tiles, first, target):
        def one(q, carry):
            made = [project(tiles, first, HALF + q * 4 + i) for i in range(4)]
            target[:, pl.ds(pl.multiple_of(q * 4 * TS, 4 * TS), 4 * TS)] = jnp.concatenate(made, axis=1)
            return carry

        lax.fori_loop(0, (FT - HALF) // 4, one, 0, unroll=2)

    def keep(tiles, first, target):
        def one(q, carry):
            made = [project(tiles, first, q * 4 + i) for i in range(4)]
            target[:, pl.ds(pl.multiple_of(q * 4 * TS, 4 * TS), 4 * TS)] = stacked(
                jnp.concatenate(made, axis=1)
            )
            return carry

        lax.fori_loop(0, HALF // 4, one, 0, unroll=2)

    total = jnp.zeros((2 * K, 2 * K), F32)
    total = lax.fori_loop(2, 4, split, total, unroll=2)
    total = lax.fori_loop(10, 12, split, total, unroll=2)
    load_west.wait()
    send_off(west, 0, proj_w)
    load_north.wait()
    send_off(north, 2 * FT, proj_n)

    pl.semaphore_wait(barrier, partners)

    def remote(source, target, at, device):
        return pltpu.make_async_remote_copy(
            src_ref=source,
            dst_ref=target,
            send_sem=send_band.at[at],
            recv_sem=recv_band.at[at],
            device_id=device,
            device_id_type=MESH,
        )

    move_e = remote(vec.at[:, pl.ds(FT * TS, WIDE)], got_e, 0, east)
    move_s = remote(vec.at[:, pl.ds(3 * FT * TS, WIDE)], got_s, 1, south)
    move_pw = remote(proj_w, got_pw, 2, west_of)
    move_pn = remote(proj_n, got_pn, 3, north_of)
    pl.when(col < COL - 1)(move_e.start)
    pl.when(col > 0)(move_pw.start)
    pl.when(row < ROW - 1)(move_s.start)
    pl.when(row > 0)(move_pn.start)

    total = lax.fori_loop(0, 2, split, total, unroll=2)
    total = lax.fori_loop(4, 10, split, total, unroll=3)
    total = lax.fori_loop(12, 16, split, total, unroll=4)
    keep(west, 0, here_w)
    keep(north, 2 * FT, here_n)

    def tile_rows(c, total):
        load_vals(c).wait()
        for i in range(PER):
            r = c * PER + i
            tiles = jnp.concatenate([vals[r, 0], vals[r, 1]], axis=1)
            left = jnp.dot(pair[r, 0:K], tiles, preferred_element_type=F32)
            right = jnp.concatenate([pair[cols_ref[0, 0, j, r]] for j in range(2)], axis=1)
            total = total + nt_dot(stacked(left), right)
        return total

    total = lax.fori_loop(0, CHUNKS, tile_rows, total)
    cross = folded(total)
    self_block = cross + cross.T
    [self_inverse] = inverses([self_block], 16)

    zeros = jnp.zeros((2 * K, 2 * K), F32)

    def here_band(left, right):
        def one(c, sums):
            part = pl.ds(pl.multiple_of(c * 512, 512), 512)
            a = left[:, part]
            b = stacked(right[:, part])
            return sums[0] + nt_dot(a, b), sums[1] + nt_dot(b, a)

        sums = lax.fori_loop(0, WIDE // 512, one, (zeros, zeros), unroll=2)
        return -folded(sums[0]), -folded(sums[1])

    def next_band(left, first):
        def one(c, sums):
            a = stacked(left[:, pl.ds(pl.multiple_of(c * 512, 512), 512)])
            b = jnp.concatenate([pair[first + c * 4 + i] for i in range(4)], axis=1)
            return sums[0] + nt_dot(a, b), sums[1] + nt_dot(b, a)

        sums = lax.fori_loop(0, (FT * TS - WIDE) // 512, one, (zeros, zeros), unroll=2)
        return -folded(sums[0]), -folded(sums[1])

    pl.when(col > 0)(move_e.wait_recv)
    west_here, west_here_t = here_band(here_w, got_e)
    west_here = jnp.where(col > 0, west_here, 0.0)
    west_here_t = jnp.where(col > 0, west_here_t, 0.0)
    pl.when(col < COL - 1)(move_pw.wait_recv)
    west_next, west_next_t = next_band(got_pw, FT + HALF)
    mine[0] = jnp.concatenate([self_block, west_next, west_here, west_next_t], axis=1)
    mine[1] = jnp.concatenate([self_inverse, west_here, west_next, west_here_t], axis=1)

    def to_row(step):
        return pltpu.make_async_remote_copy(
            src_ref=mine.at[(step - 1) % 2],
            dst_ref=slots.at[step - 1],
            send_sem=send_row.at[step - 1],
            recv_sem=recv_row.at[step - 1],
            device_id={"gy": lax.rem(col + step, COL)},
            device_id_type=MESH,
        )

    for step in range(1, COL):
        @pl.when(col + step < COL)
        def _():
            to_row(step).start()

    pl.when(row < ROW - 1)(move_pn.wait_recv)
    sent_n[:, 0:K] = next_band(got_pn, 3 * FT + HALF)[0]
    move_n = pltpu.make_async_remote_copy(
        src_ref=sent_n, dst_ref=got_n, send_sem=send_n, recv_sem=recv_n,
        device_id=south, device_id_type=MESH,
    )
    pl.when(row < ROW - 1)(move_n.start)

    pl.when(row > 0)(move_s.wait_recv)
    north_here = here_band(here_n, got_s)[0]
    pl.when(row > 0)(move_n.wait_recv)
    north_block = jnp.where(row > 0, north_here + got_n[:, 0:K], 0.0)
    out_ref[COL - 1] = jnp.concatenate(
        [self_block, west_here, north_block, jnp.zeros((K, K), F32)], axis=1
    )

    for step in range(1, COL):
        @pl.when(col >= step)
        def _():
            to_row(step).wait_recv()
            out_ref[step - 1] = slots[step - 1]

        @pl.when(col < step)
        def _():
            out_ref[step - 1] = jnp.zeros((K, 4 * K), F32)

        @pl.when(col + step < COL)
        def _():
            to_row(step).wait_send()

    pl.when(col < COL - 1)(move_e.wait_send)
    pl.when(row < ROW - 1)(move_s.wait_send)
    pl.when(col > 0)(move_pw.wait_send)
    pl.when(row > 0)(move_pn.wait_send)
    pl.when(row < ROW - 1)(move_n.wait_send)


def made_blocks(defl, diag, vals, cols, west, north):
    hbm = pl.BlockSpec(memory_space=pl.ANY)
    vmem = pl.BlockSpec(memory_space=pltpu.VMEM)
    return pl.pallas_call(
        blocks_kernel,
        out_shape=jax.ShapeDtypeStruct((COL, K, 4 * K), F32),
        in_specs=[hbm, vmem, hbm, pl.BlockSpec(memory_space=pltpu.SMEM), hbm, hbm],
        out_specs=vmem,
        scratch_shapes=[
            pltpu.VMEM((K, NL), F32),
            pltpu.VMEM((NT, 2 * K, TS), BF16),
            pltpu.VMEM((NT, 2, TS, TS), BF16),
            pltpu.VMEM((FT, TS, TS), BF16),
            pltpu.VMEM((FT, TS, TS), BF16),
            pltpu.VMEM((2 * K, WIDE), BF16),
            pltpu.VMEM((2 * K, WIDE), BF16),
            pltpu.VMEM((K, FT * TS - WIDE), F32),
            pltpu.VMEM((K, FT * TS - WIDE), F32),
            pltpu.VMEM((K, WIDE), F32),
            pltpu.VMEM((K, WIDE), F32),
            pltpu.VMEM((K, FT * TS - WIDE), F32),
            pltpu.VMEM((K, FT * TS - WIDE), F32),
            pltpu.VMEM((2, K, 4 * K), F32),
            pltpu.VMEM((COL - 1, K, 4 * K), F32),
            pltpu.VMEM((K, 4 * K), F32),
            pltpu.VMEM((K, 4 * K), F32),
            pltpu.SemaphoreType.DMA((3,)),
            pltpu.SemaphoreType.DMA((CHUNKS,)),
            pltpu.SemaphoreType.DMA((4,)),
            pltpu.SemaphoreType.DMA((4,)),
            pltpu.SemaphoreType.DMA((COL - 1,)),
            pltpu.SemaphoreType.DMA((COL - 1,)),
            pltpu.SemaphoreType.DMA,
            pltpu.SemaphoreType.DMA,
        ],
        compiler_params=pltpu.CompilerParams(
            collective_id=0, has_side_effects=True, vmem_limit_bytes=60 * 2**20
        ),
    )(defl, diag, vals, cols, west, north)


def inverse(packs, width):
    shape = (K, 4 * K)
    lane = lax.broadcasted_iota(jnp.int32, shape, 1)
    sub = lax.broadcasted_iota(jnp.int32, shape, 0)
    within = lax.rem(lane, K)
    base = lane - within
    packs = list(packs)
    for first in range(0, K, width):
        panels = [
            [jnp.take_along_axis(m, base + (first + q), axis=1) for q in range(width)]
            for m in packs
        ]
        for q in range(width):
            k = first + q
            is_row = sub == k
            is_lane = within == k
            for at, m in enumerate(packs):
                panel = panels[at]
                column = panel[q]
                scale = 1.0 / column[k : k + 1]
                for later in range(q + 1, width):
                    part = panel[later][k : k + 1] * scale
                    panel[later] = jnp.where(is_row, part, panel[later] - column * part)
                line = jnp.where(is_lane[0:1], 1.0, m[k : k + 1]) * scale
                packs[at] = jnp.where(is_row, line, jnp.where(is_lane, 0.0, m) - column * line)
    return packs


NODES = COL - 1


def chain_kernel(got_ref, coarse_ref, pivot_ref, mult_ref, nodes, links, turned):
    col = lax.axis_index("gy")
    own = got_ref[COL - 1]
    self_own = own[:, 0:K]
    west_own = (own + got_ref[0])[:, K : 2 * K]
    west_own = jnp.where(col > 0, west_own, 0.0)
    coarse_ref[0, 0, 0] = self_own
    coarse_ref[0, 0, 1] = west_own
    coarse_ref[0, 0, 2] = own[:, 2 * K : 3 * K]
    eye = (
        lax.broadcasted_iota(jnp.int32, (K, K), 0) == lax.broadcasted_iota(jnp.int32, (K, K), 1)
    ).astype(F32)
    nodes[0] = jnp.where(col > 0, got_ref[0][:, 0:K], eye)

    def eliminate(stride, held, gone, links_now, solved):
        for k, inv in zip(gone, solved, strict=True):
            near = links_now[k - stride][0]
            if k + stride < NODES:
                far, far_t = links_now[k]
                outer = exact(jnp.concatenate([near, far_t], axis=0), inv)
                to_near = exact_nt(outer, near)
                to_far = exact(outer, far)
                held[k - stride] = held[k - stride] - to_near[0:K]
                held[k + stride] = held[k + stride] - to_far[K : 2 * K]
                links[k - stride] = -to_far[0:K]
                turned[k - stride] = -to_near[K : 2 * K]
            else:
                held[k - stride] = held[k - stride] - exact_nt(exact(near, inv), near)
        for k in range(0, NODES, 2 * stride):
            nodes[k] = held[k]

    @pl.when(col > 1)
    def _():
        held = {k: jnp.where(k < col, got_ref[k][:, 0:K], eye) for k in range(0, NODES, 2)}
        links_now = {}
        for k in range(NODES - 1):
            both = got_ref[k] + got_ref[k + 1]
            if k % 2:
                links_now[k] = (both[:, K : 2 * K], both[:, 3 * K : 4 * K])
            else:
                links_now[k] = (both[:, 2 * K : 3 * K],)
        gone = list(range(1, NODES, 2))
        eliminate(1, held, gone, links_now, [got_ref[k][:, 0:K] for k in gone])

    def level(stride):
        held = {k: nodes[k] for k in range(0, NODES, stride)}
        links_now = {k: (links[k], turned[k]) for k in range(0, NODES - stride, stride)}
        gone = list(range(stride, NODES, 2 * stride))
        if len(gone) == 4:
            [pack] = inverse([jnp.concatenate([held[k] for k in gone], axis=1)], 16)
            solved = [pack[:, at * K : (at + 1) * K] for at in range(4)]
        else:
            solved = inverses([held[k] for k in gone], 16)
        eliminate(stride, held, gone, links_now, solved)

    for stride in (2, 4, 8):
        pl.when(col > stride)(functools.partial(level, stride))
    [last] = inverses([nodes[0]], 16)
    mult = exact(west_own, last)
    pivot_ref[0, 0] = self_own - exact_nt(mult, west_own)
    mult_ref[0, 0] = mult


def local(defl, diag, vals, cols, west, north):
    got = made_blocks(defl, diag, vals, jnp.swapaxes(cols, 2, 3), west, north)
    vmem = pl.BlockSpec(memory_space=pltpu.VMEM)
    return pl.pallas_call(
        chain_kernel,
        out_shape=(
            jax.ShapeDtypeStruct((1, 1, 3, K, K), F32),
            jax.ShapeDtypeStruct((1, 1, K, K), F32),
            jax.ShapeDtypeStruct((1, 1, K, K), F32),
        ),
        in_specs=[vmem],
        out_specs=(vmem, vmem, vmem),
        scratch_shapes=[pltpu.VMEM((NODES, K, K), F32)] * 3,
        compiler_params=pltpu.CompilerParams(vmem_limit_bytes=16 * 2**20),
    )(got)


def solution(mesh):
    placed = (
        P("gx", "gy", None, None),
        P("gx", "gy", None),
        P("gx", "gy", None, None, None, None),
        P("gx", "gy", None, None),
        P("gx", "gy", None, None, None),
        P("gx", "gy", None, None, None),
    )
    return jax.shard_map(
        local,
        mesh=mesh,
        in_specs=placed,
        out_specs=(
            P("gx", "gy", None, None, None),
            P("gx", "gy", None, None),
            P("gx", "gy", None, None),
        ),
        check_vma=False,
    )
```

```python
import functools

import jax
import jax.numpy as jnp
from jax import lax
from jax.experimental import pallas as pl
from jax.experimental.pallas import tpu as pltpu
from jax.sharding import PartitionSpec as P

MESH = pl.DeviceIdType.MESH
F32 = jnp.float32
BF16 = jnp.bfloat16
HIGHEST = lax.Precision.HIGHEST

K = 32
TS = 128
NT = 128
FT = 32
NL = NT * TS
ROW = 16
COL = 16
HALF = 16
WIDE = HALF * TS
CHUNKS = 8
PER = NT // CHUNKS
NT_DIMS = (((1,), (1,)), ((), ()))


def halves(values):
    high = values.astype(BF16)
    low = (values - high.astype(F32)).astype(BF16)
    return high, low


def stacked(values):
    high, low = halves(values)
    return jnp.concatenate([high, low], axis=0)


def folded(total):
    return (
        total[0:K, 0:K] + total[0:K, K : 2 * K] + total[K : 2 * K, 0:K] + total[K : 2 * K, K : 2 * K]
    )


def nt_dot(left, right):
    return lax.dot_general(left, right, NT_DIMS, preferred_element_type=F32)


def exact(left, right):
    return jnp.dot(left, right, precision=HIGHEST, preferred_element_type=F32)


def exact_nt(left, right):
    return lax.dot_general(left, right, NT_DIMS, precision=HIGHEST, preferred_element_type=F32)


def inverses(blocks, width):
    lane = lax.broadcasted_iota(jnp.int32, (K, K), 1)
    sub = lax.broadcasted_iota(jnp.int32, (K, K), 0)
    blocks = list(blocks)
    for first in range(0, K, width):
        panels = [
            [jnp.broadcast_to(m[:, first + q : first + q + 1], (K, K)) for q in range(width)]
            for m in blocks
        ]
        for q in range(width):
            k = first + q
            is_row = sub == k
            is_lane = lane == k
            for at, m in enumerate(blocks):
                panel = panels[at]
                column = panel[q]
                scale = 1.0 / column[k : k + 1]
                for later in range(q + 1, width):
                    part = panel[later][k : k + 1] * scale
                    panel[later] = jnp.where(is_row, part, panel[later] - column * part)
                line = jnp.where(is_lane[0:1], 1.0, m[k : k + 1]) * scale
                blocks[at] = jnp.where(is_row, line, jnp.where(is_lane, 0.0, m) - column * line)
    return blocks


def blocks_kernel(
    defl_hbm, diag_ref, vals_hbm, cols_ref, west_hbm, north_hbm,
    out_ref,
    vec, pair, vals, west, north, here_w, here_n, proj_w, proj_n,
    got_e, got_s, got_pw, got_pn, mine, slots, got_n, sent_n,
    sem_in, sem_vals, send_band, recv_band, send_row, recv_row, send_n, recv_n,
):
    row = lax.axis_index("gx")
    col = lax.axis_index("gy")
    east = {"gy": lax.rem(col + 1, COL)}
    west_of = {"gy": lax.rem(col + COL - 1, COL)}
    south = {"gx": lax.rem(row + 1, ROW)}
    north_of = {"gx": lax.rem(row + ROW - 1, ROW)}

    load_vec = pltpu.make_async_copy(defl_hbm.at[0, 0], vec, sem_in.at[0])
    load_west = pltpu.make_async_copy(west_hbm.at[0, 0], west, sem_in.at[1])
    load_north = pltpu.make_async_copy(north_hbm.at[0, 0], north, sem_in.at[2])
    load_vec.start()
    load_west.start()
    load_north.start()

    barrier = pltpu.get_barrier_semaphore()

    def greet(there, device):
        @pl.when(there)
        def _():
            pl.semaphore_signal(barrier, inc=1, device_id=device, device_id_type=MESH)

    for step in range(1, COL):
        greet(col >= step, {"gy": lax.rem(col + COL - step, COL)})
    greet(col < COL - 1, east)
    greet(row < ROW - 1, south)
    greet(row > 0, north_of)
    partners = (
        (COL - 1 - col)
        + jnp.where(col > 0, 1, 0)
        + jnp.where(row < ROW - 1, 1, 0)
        + jnp.where(row > 0, 1, 0)
    )

    def load_vals(c):
        part = pl.ds(c * PER, PER)
        return pltpu.make_async_copy(vals_hbm.at[0, 0, part], vals.at[part], sem_vals.at[c])

    load_vec.wait()
    for c in range(CHUNKS):
        load_vals(c).start()

    def split(c, total):
        part = pl.ds(pl.multiple_of(c * 1024, 1024), 1024)
        values = vec[:, part]
        both = stacked(values)
        for t in range(8):
            pair[c * 8 + t] = both[:, t * TS : (t + 1) * TS]
        scaled = stacked(values * (diag_ref[0, :, part] * 0.5))
        return total + nt_dot(scaled, both)

    def project(tiles, first, f):
        return jnp.dot(pair[first + f, 0:K], tiles[f], preferred_element_type=F32)

    def send_off(tiles, first, target):
        def one(q, carry):
            made = [project(tiles, first, HALF + q * 4 + i) for i in range(4)]
            target[:, pl.ds(pl.multiple_of(q * 4 * TS, 4 * TS), 4 * TS)] = jnp.concatenate(made, axis=1)
            return carry

        lax.fori_loop(0, (FT - HALF) // 4, one, 0, unroll=2)

    def keep(tiles, first, target):
        def one(q, carry):
            made = [project(tiles, first, q * 4 + i) for i in range(4)]
            target[:, pl.ds(pl.multiple_of(q * 4 * TS, 4 * TS), 4 * TS)] = stacked(
                jnp.concatenate(made, axis=1)
            )
            return carry

        lax.fori_loop(0, HALF // 4, one, 0, unroll=2)

    total = jnp.zeros((2 * K, 2 * K), F32)
    total = lax.fori_loop(2, 4, split, total, unroll=2)
    total = lax.fori_loop(10, 12, split, total, unroll=2)
    load_west.wait()
    send_off(west, 0, proj_w)
    load_north.wait()
    send_off(north, 2 * FT, proj_n)

    pl.semaphore_wait(barrier, partners)

    def remote(source, target, at, device):
        return pltpu.make_async_remote_copy(
            src_ref=source,
            dst_ref=target,
            send_sem=send_band.at[at],
            recv_sem=recv_band.at[at],
            device_id=device,
            device_id_type=MESH,
        )

    move_e = remote(vec.at[:, pl.ds(FT * TS, WIDE)], got_e, 0, east)
    move_s = remote(vec.at[:, pl.ds(3 * FT * TS, WIDE)], got_s, 1, south)
    move_pw = remote(proj_w, got_pw, 2, west_of)
    move_pn = remote(proj_n, got_pn, 3, north_of)
    pl.when(col < COL - 1)(move_e.start)
    pl.when(col > 0)(move_pw.start)
    pl.when(row < ROW - 1)(move_s.start)
    pl.when(row > 0)(move_pn.start)

    total = lax.fori_loop(0, 2, split, total, unroll=2)
    total = lax.fori_loop(4, 10, split, total, unroll=3)
    total = lax.fori_loop(12, 16, split, total, unroll=4)
    keep(west, 0, here_w)
    keep(north, 2 * FT, here_n)

    def tile_rows(c, total):
        load_vals(c).wait()
        for i in range(PER):
            r = c * PER + i
            tiles = jnp.concatenate([vals[r, 0], vals[r, 1]], axis=1)
            left = jnp.dot(pair[r, 0:K], tiles, preferred_element_type=F32)
            right = jnp.concatenate([pair[cols_ref[0, 0, j, r]] for j in range(2)], axis=1)
            total = total + nt_dot(stacked(left), right)
        return total

    total = lax.fori_loop(0, CHUNKS, tile_rows, total)
    cross = folded(total)
    self_block = cross + cross.T
    [self_inverse] = inverses([self_block], 16)

    zeros = jnp.zeros((2 * K, 2 * K), F32)

    def here_band(left, right):
        def one(c, sums):
            part = pl.ds(pl.multiple_of(c * 512, 512), 512)
            a = left[:, part]
            b = stacked(right[:, part])
            return sums[0] + nt_dot(a, b), sums[1] + nt_dot(b, a)

        sums = lax.fori_loop(0, WIDE // 512, one, (zeros, zeros), unroll=4)
        return -folded(sums[0]), -folded(sums[1])

    def next_band(left, first):
        def one(c, sums):
            a = stacked(left[:, pl.ds(pl.multiple_of(c * 512, 512), 512)])
            b = jnp.concatenate([pair[first + c * 4 + i] for i in range(4)], axis=1)
            return sums[0] + nt_dot(a, b), sums[1] + nt_dot(b, a)

        sums = lax.fori_loop(0, (FT * TS - WIDE) // 512, one, (zeros, zeros), unroll=4)
        return -folded(sums[0]), -folded(sums[1])

    pl.when(col > 0)(move_e.wait_recv)
    west_here, west_here_t = here_band(here_w, got_e)
    west_here = jnp.where(col > 0, west_here, 0.0)
    west_here_t = jnp.where(col > 0, west_here_t, 0.0)
    pl.when(col < COL - 1)(move_pw.wait_recv)
    west_next, west_next_t = next_band(got_pw, FT + HALF)
    mine[0] = jnp.concatenate([self_block, west_next, west_here, west_next_t], axis=1)
    mine[1] = jnp.concatenate([self_inverse, west_here, west_next, west_here_t], axis=1)

    def to_row(step):
        return pltpu.make_async_remote_copy(
            src_ref=mine.at[(step - 1) % 2],
            dst_ref=slots.at[step - 1],
            send_sem=send_row.at[step - 1],
            recv_sem=recv_row.at[step - 1],
            device_id={"gy": lax.rem(col + step, COL)},
            device_id_type=MESH,
        )

    for step in range(1, COL):
        @pl.when(col + step < COL)
        def _():
            to_row(step).start()

    pl.when(row < ROW - 1)(move_pn.wait_recv)
    sent_n[:, 0:K] = next_band(got_pn, 3 * FT + HALF)[0]
    move_n = pltpu.make_async_remote_copy(
        src_ref=sent_n, dst_ref=got_n, send_sem=send_n, recv_sem=recv_n,
        device_id=south, device_id_type=MESH,
    )
    pl.when(row < ROW - 1)(move_n.start)

    pl.when(row > 0)(move_s.wait_recv)
    north_here = here_band(here_n, got_s)[0]
    pl.when(row > 0)(move_n.wait_recv)
    north_block = jnp.where(row > 0, north_here + got_n[:, 0:K], 0.0)
    out_ref[COL - 1] = jnp.concatenate(
        [self_block, west_here, north_block, jnp.zeros((K, K), F32)], axis=1
    )

    for step in range(1, COL):
        @pl.when(col >= step)
        def _():
            to_row(step).wait_recv()
            out_ref[step - 1] = slots[step - 1]

        @pl.when(col < step)
        def _():
            out_ref[step - 1] = jnp.zeros((K, 4 * K), F32)

        @pl.when(col + step < COL)
        def _():
            to_row(step).wait_send()

    pl.when(col < COL - 1)(move_e.wait_send)
    pl.when(row < ROW - 1)(move_s.wait_send)
    pl.when(col > 0)(move_pw.wait_send)
    pl.when(row > 0)(move_pn.wait_send)
    pl.when(row < ROW - 1)(move_n.wait_send)


def made_blocks(defl, diag, vals, cols, west, north):
    hbm = pl.BlockSpec(memory_space=pl.ANY)
    vmem = pl.BlockSpec(memory_space=pltpu.VMEM)
    return pl.pallas_call(
        blocks_kernel,
        out_shape=pltpu.VMEM((COL, K, 4 * K), F32),
        in_specs=[hbm, vmem, hbm, pl.BlockSpec(memory_space=pltpu.SMEM), hbm, hbm],
        out_specs=vmem,
        scratch_shapes=[
            pltpu.VMEM((K, NL), F32),
            pltpu.VMEM((NT, 2 * K, TS), BF16),
            pltpu.VMEM((NT, 2, TS, TS), BF16),
            pltpu.VMEM((FT, TS, TS), BF16),
            pltpu.VMEM((FT, TS, TS), BF16),
            pltpu.VMEM((2 * K, WIDE), BF16),
            pltpu.VMEM((2 * K, WIDE), BF16),
            pltpu.VMEM((K, FT * TS - WIDE), F32),
            pltpu.VMEM((K, FT * TS - WIDE), F32),
            pltpu.VMEM((K, WIDE), F32),
            pltpu.VMEM((K, WIDE), F32),
            pltpu.VMEM((K, FT * TS - WIDE), F32),
            pltpu.VMEM((K, FT * TS - WIDE), F32),
            pltpu.VMEM((2, K, 4 * K), F32),
            pltpu.VMEM((COL - 1, K, 4 * K), F32),
            pltpu.VMEM((K, 4 * K), F32),
            pltpu.VMEM((K, 4 * K), F32),
            pltpu.SemaphoreType.DMA((3,)),
            pltpu.SemaphoreType.DMA((CHUNKS,)),
            pltpu.SemaphoreType.DMA((4,)),
            pltpu.SemaphoreType.DMA((4,)),
            pltpu.SemaphoreType.DMA((COL - 1,)),
            pltpu.SemaphoreType.DMA((COL - 1,)),
            pltpu.SemaphoreType.DMA,
            pltpu.SemaphoreType.DMA,
        ],
        compiler_params=pltpu.CompilerParams(
            collective_id=0, has_side_effects=True, vmem_limit_bytes=60 * 2**20
        ),
    )(defl, diag, vals, cols, west, north)


NODES = COL - 1


def chain_kernel(got_ref, coarse_ref, pivot_ref, mult_ref, nodes, links, turned):
    col = lax.axis_index("gy")
    own = got_ref[COL - 1]
    self_own = own[:, 0:K]
    west_own = (own + got_ref[0])[:, K : 2 * K]
    west_own = jnp.where(col > 0, west_own, 0.0)
    coarse_ref[0, 0, 0] = self_own
    coarse_ref[0, 0, 1] = west_own
    coarse_ref[0, 0, 2] = own[:, 2 * K : 3 * K]
    eye = (
        lax.broadcasted_iota(jnp.int32, (K, K), 0) == lax.broadcasted_iota(jnp.int32, (K, K), 1)
    ).astype(F32)
    nodes[0] = jnp.where(col > 0, got_ref[0][:, 0:K], eye)

    def eliminate(stride, held, gone, links_now, solved):
        for k, inv in zip(gone, solved, strict=True):
            near = links_now[k - stride][0]
            if k + stride < NODES:
                far, far_t = links_now[k]
                outer = exact(jnp.concatenate([near, far_t], axis=0), inv)
                to_near = exact_nt(outer, near)
                to_far = exact(outer, far)
                held[k - stride] = held[k - stride] - to_near[0:K]
                held[k + stride] = held[k + stride] - to_far[K : 2 * K]
                links[k - stride] = -to_far[0:K]
                turned[k - stride] = -to_near[K : 2 * K]
            else:
                held[k - stride] = held[k - stride] - exact_nt(exact(near, inv), near)
        for k in range(0, NODES, 2 * stride):
            nodes[k] = held[k]

    @pl.when(col > 1)
    def _():
        held = {k: jnp.where(k < col, got_ref[k][:, 0:K], eye) for k in range(0, NODES, 2)}
        links_now = {}
        for k in range(NODES - 1):
            both = got_ref[k] + got_ref[k + 1]
            if k % 2:
                links_now[k] = (both[:, K : 2 * K], both[:, 3 * K : 4 * K])
            else:
                links_now[k] = (both[:, 2 * K : 3 * K],)
        gone = list(range(1, NODES, 2))
        eliminate(1, held, gone, links_now, [got_ref[k][:, 0:K] for k in gone])

    def level(stride):
        held = {k: nodes[k] for k in range(0, NODES, stride)}
        links_now = {k: (links[k], turned[k]) for k in range(0, NODES - stride, stride)}
        gone = list(range(stride, NODES, 2 * stride))
        solved = inverses([held[k] for k in gone], 8)
        eliminate(stride, held, gone, links_now, solved)

    for stride in (2, 4, 8):
        pl.when(col > stride)(functools.partial(level, stride))
    [last] = inverses([nodes[0]], 16)
    mult = exact(west_own, last)
    pivot_ref[0, 0] = self_own - exact_nt(mult, west_own)
    mult_ref[0, 0] = mult


def local(defl, diag, vals, cols, west, north):
    got = made_blocks(defl, diag, vals, jnp.swapaxes(cols, 2, 3), west, north)
    vmem = pl.BlockSpec(memory_space=pltpu.VMEM)
    return pl.pallas_call(
        chain_kernel,
        out_shape=(
            jax.ShapeDtypeStruct((1, 1, 3, K, K), F32),
            jax.ShapeDtypeStruct((1, 1, K, K), F32),
            jax.ShapeDtypeStruct((1, 1, K, K), F32),
        ),
        in_specs=[vmem],
        out_specs=(vmem, vmem, vmem),
        scratch_shapes=[pltpu.VMEM((NODES, K, K), F32)] * 3,
        compiler_params=pltpu.CompilerParams(vmem_limit_bytes=16 * 2**20),
    )(got)


def solution(mesh):
    placed = (
        P("gx", "gy", None, None),
        P("gx", "gy", None),
        P("gx", "gy", None, None, None, None),
        P("gx", "gy", None, None),
        P("gx", "gy", None, None, None),
        P("gx", "gy", None, None, None),
    )
    return jax.shard_map(
        local,
        mesh=mesh,
        in_specs=placed,
        out_specs=(
            P("gx", "gy", None, None, None),
            P("gx", "gy", None, None),
            P("gx", "gy", None, None),
        ),
        check_vma=False,
    )
```

```python
import functools

import jax
import jax.numpy as jnp
from jax import lax
from jax.experimental import pallas as pl
from jax.experimental.pallas import tpu as pltpu
from jax.sharding import PartitionSpec as P

MESH = pl.DeviceIdType.MESH
F32 = jnp.float32
BF16 = jnp.bfloat16
HIGHEST = lax.Precision.HIGHEST

K = 32
TS = 128
NT = 128
FT = 32
NL = NT * TS
ROW = 16
COL = 16
HALF = 16
WIDE = HALF * TS
CHUNKS = 8
PER = NT // CHUNKS
NT_DIMS = (((1,), (1,)), ((), ()))


def halves(values):
    high = values.astype(BF16)
    low = (values - high.astype(F32)).astype(BF16)
    return high, low


def stacked(values):
    high, low = halves(values)
    return jnp.concatenate([high, low], axis=0)


def folded(total):
    return (
        total[0:K, 0:K] + total[0:K, K : 2 * K] + total[K : 2 * K, 0:K] + total[K : 2 * K, K : 2 * K]
    )


def nt_dot(left, right):
    return lax.dot_general(left, right, NT_DIMS, preferred_element_type=F32)


def exact(left, right):
    return jnp.dot(left, right, precision=HIGHEST, preferred_element_type=F32)


def exact_nt(left, right):
    return lax.dot_general(left, right, NT_DIMS, precision=HIGHEST, preferred_element_type=F32)


def inverses(blocks, width):
    lane = lax.broadcasted_iota(jnp.int32, (K, K), 1)
    sub = lax.broadcasted_iota(jnp.int32, (K, K), 0)
    blocks = list(blocks)
    for first in range(0, K, width):
        panels = [
            [jnp.broadcast_to(m[:, first + q : first + q + 1], (K, K)) for q in range(width)]
            for m in blocks
        ]
        for q in range(width):
            k = first + q
            is_row = sub == k
            is_lane = lane == k
            for at, m in enumerate(blocks):
                panel = panels[at]
                column = panel[q]
                scale = 1.0 / column[k : k + 1]
                for later in range(q + 1, width):
                    part = panel[later][k : k + 1] * scale
                    panel[later] = jnp.where(is_row, part, panel[later] - column * part)
                line = jnp.where(is_lane[0:1], 1.0, m[k : k + 1]) * scale
                blocks[at] = jnp.where(is_row, line, jnp.where(is_lane, 0.0, m) - column * line)
    return blocks


def blocks_kernel(
    defl_hbm, diag_ref, vals_hbm, cols_ref, west_hbm, north_hbm,
    out_ref,
    vec, pair, vals, west, north, here_w, here_n, proj_w, proj_n,
    got_e, got_s, got_pw, got_pn, mine, slots, got_n, sent_n,
    sem_in, sem_vals, send_band, recv_band, send_row, recv_row, send_n, recv_n,
):
    row = lax.axis_index("gx")
    col = lax.axis_index("gy")
    east = {"gy": lax.rem(col + 1, COL)}
    west_of = {"gy": lax.rem(col + COL - 1, COL)}
    south = {"gx": lax.rem(row + 1, ROW)}
    north_of = {"gx": lax.rem(row + ROW - 1, ROW)}

    load_vec = pltpu.make_async_copy(defl_hbm.at[0, 0], vec, sem_in.at[0])
    load_west = pltpu.make_async_copy(west_hbm.at[0, 0], west, sem_in.at[1])
    load_north = pltpu.make_async_copy(north_hbm.at[0, 0], north, sem_in.at[2])
    load_vec.start()
    load_west.start()
    load_north.start()

    barrier = pltpu.get_barrier_semaphore()

    def greet(there, device):
        @pl.when(there)
        def _():
            pl.semaphore_signal(barrier, inc=1, device_id=device, device_id_type=MESH)

    for step in range(1, COL):
        greet(col >= step, {"gy": lax.rem(col + COL - step, COL)})
    greet(col < COL - 1, east)
    greet(row < ROW - 1, south)
    greet(row > 0, north_of)
    partners = (
        (COL - 1 - col)
        + jnp.where(col > 0, 1, 0)
        + jnp.where(row < ROW - 1, 1, 0)
        + jnp.where(row > 0, 1, 0)
    )

    def load_vals(c):
        part = pl.ds(c * PER, PER)
        return pltpu.make_async_copy(vals_hbm.at[0, 0, part], vals.at[part], sem_vals.at[c])

    load_vec.wait()
    for c in range(CHUNKS):
        load_vals(c).start()

    def split(c, total):
        part = pl.ds(pl.multiple_of(c * 1024, 1024), 1024)
        values = vec[:, part]
        both = stacked(values)
        for t in range(8):
            pair[c * 8 + t] = both[:, t * TS : (t + 1) * TS]
        scaled = stacked(values * (diag_ref[0, :, part] * 0.5))
        return total + nt_dot(scaled, both)

    def project(tiles, first, f):
        return jnp.dot(pair[first + f, 0:K], tiles[f], preferred_element_type=F32)

    def send_off(tiles, first, target):
        def one(q, carry):
            made = [project(tiles, first, HALF + q * 4 + i) for i in range(4)]
            target[:, pl.ds(pl.multiple_of(q * 4 * TS, 4 * TS), 4 * TS)] = jnp.concatenate(made, axis=1)
            return carry

        lax.fori_loop(0, (FT - HALF) // 4, one, 0, unroll=2)

    def keep(tiles, first, target):
        def one(q, carry):
            made = [project(tiles, first, q * 4 + i) for i in range(4)]
            target[:, pl.ds(pl.multiple_of(q * 4 * TS, 4 * TS), 4 * TS)] = stacked(
                jnp.concatenate(made, axis=1)
            )
            return carry

        lax.fori_loop(0, HALF // 4, one, 0, unroll=2)

    total = jnp.zeros((2 * K, 2 * K), F32)
    total = lax.fori_loop(2, 4, split, total, unroll=2)
    total = lax.fori_loop(10, 12, split, total, unroll=2)
    load_west.wait()
    send_off(west, 0, proj_w)
    load_north.wait()
    send_off(north, 2 * FT, proj_n)

    pl.semaphore_wait(barrier, partners)

    def remote(source, target, at, device):
        return pltpu.make_async_remote_copy(
            src_ref=source,
            dst_ref=target,
            send_sem=send_band.at[at],
            recv_sem=recv_band.at[at],
            device_id=device,
            device_id_type=MESH,
        )

    move_e = remote(vec.at[:, pl.ds(FT * TS, WIDE)], got_e, 0, east)
    move_s = remote(vec.at[:, pl.ds(3 * FT * TS, WIDE)], got_s, 1, south)
    move_pw = remote(proj_w, got_pw, 2, west_of)
    move_pn = remote(proj_n, got_pn, 3, north_of)
    pl.when(col < COL - 1)(move_e.start)
    pl.when(col > 0)(move_pw.start)
    pl.when(row < ROW - 1)(move_s.start)
    pl.when(row > 0)(move_pn.start)

    total = lax.fori_loop(0, 2, split, total, unroll=2)
    total = lax.fori_loop(4, 10, split, total, unroll=3)
    total = lax.fori_loop(12, 16, split, total, unroll=4)
    keep(west, 0, here_w)
    keep(north, 2 * FT, here_n)

    def tile_rows(c, total):
        load_vals(c).wait()
        for i in range(PER):
            r = c * PER + i
            tiles = jnp.concatenate([vals[r, 0], vals[r, 1]], axis=1)
            left = jnp.dot(pair[r, 0:K], tiles, preferred_element_type=F32)
            right = jnp.concatenate([pair[cols_ref[0, 0, j, r]] for j in range(2)], axis=1)
            total = total + nt_dot(stacked(left), right)
        return total

    total = lax.fori_loop(0, CHUNKS, tile_rows, total)
    cross = folded(total)
    self_block = cross + cross.T
    [self_inverse] = inverses([self_block], 16)

    zeros = jnp.zeros((2 * K, 2 * K), F32)

    def here_band(left, right):
        def one(c, sums):
            part = pl.ds(pl.multiple_of(c * 512, 512), 512)
            a = left[:, part]
            b = stacked(right[:, part])
            return sums[0] + nt_dot(a, b), sums[1] + nt_dot(b, a)

        sums = lax.fori_loop(0, WIDE // 512, one, (zeros, zeros), unroll=4)
        return -folded(sums[0]), -folded(sums[1])

    def next_band(left, first):
        def one(c, sums):
            a = stacked(left[:, pl.ds(pl.multiple_of(c * 512, 512), 512)])
            b = jnp.concatenate([pair[first + c * 4 + i] for i in range(4)], axis=1)
            return sums[0] + nt_dot(a, b), sums[1] + nt_dot(b, a)

        sums = lax.fori_loop(0, (FT * TS - WIDE) // 512, one, (zeros, zeros), unroll=4)
        return -folded(sums[0]), -folded(sums[1])

    pl.when(col > 0)(move_e.wait_recv)
    west_here, west_here_t = here_band(here_w, got_e)
    west_here = jnp.where(col > 0, west_here, 0.0)
    west_here_t = jnp.where(col > 0, west_here_t, 0.0)
    pl.when(col < COL - 1)(move_pw.wait_recv)
    west_next, west_next_t = next_band(got_pw, FT + HALF)
    mine[0] = jnp.concatenate([self_block, west_next, west_here, west_next_t], axis=1)
    mine[1] = jnp.concatenate([self_inverse, west_here, west_next, west_here_t], axis=1)

    def to_row(step):
        return pltpu.make_async_remote_copy(
            src_ref=mine.at[(step - 1) % 2],
            dst_ref=slots.at[step - 1],
            send_sem=send_row.at[step - 1],
            recv_sem=recv_row.at[step - 1],
            device_id={"gy": lax.rem(col + step, COL)},
            device_id_type=MESH,
        )

    for step in range(1, COL):
        @pl.when(col + step < COL)
        def _():
            to_row(step).start()

    pl.when(row < ROW - 1)(move_pn.wait_recv)
    sent_n[:, 0:K] = next_band(got_pn, 3 * FT + HALF)[0]
    move_n = pltpu.make_async_remote_copy(
        src_ref=sent_n, dst_ref=got_n, send_sem=send_n, recv_sem=recv_n,
        device_id=south, device_id_type=MESH,
    )
    pl.when(row < ROW - 1)(move_n.start)

    pl.when(row > 0)(move_s.wait_recv)
    north_here = here_band(here_n, got_s)[0]
    pl.when(row > 0)(move_n.wait_recv)
    north_block = jnp.where(row > 0, north_here + got_n[:, 0:K], 0.0)
    out_ref[COL - 1] = jnp.concatenate(
        [self_block, west_here, north_block, jnp.zeros((K, K), F32)], axis=1
    )

    for step in range(1, COL):
        @pl.when(col >= step)
        def _():
            to_row(step).wait_recv()
            out_ref[step - 1] = slots[step - 1]

        @pl.when(col < step)
        def _():
            out_ref[step - 1] = jnp.zeros((K, 4 * K), F32)

        @pl.when(col + step < COL)
        def _():
            to_row(step).wait_send()

    pl.when(col < COL - 1)(move_e.wait_send)
    pl.when(row < ROW - 1)(move_s.wait_send)
    pl.when(col > 0)(move_pw.wait_send)
    pl.when(row > 0)(move_pn.wait_send)
    pl.when(row < ROW - 1)(move_n.wait_send)


def made_blocks(defl, diag, vals, cols, west, north):
    hbm = pl.BlockSpec(memory_space=pl.ANY)
    vmem = pl.BlockSpec(memory_space=pltpu.VMEM)
    return pl.pallas_call(
        blocks_kernel,
        out_shape=pltpu.VMEM((COL, K, 4 * K), F32),
        in_specs=[hbm, vmem, hbm, pl.BlockSpec(memory_space=pltpu.SMEM), hbm, hbm],
        out_specs=vmem,
        scratch_shapes=[
            pltpu.VMEM((K, NL), F32),
            pltpu.VMEM((NT, 2 * K, TS), BF16),
            pltpu.VMEM((NT, 2, TS, TS), BF16),
            pltpu.VMEM((FT, TS, TS), BF16),
            pltpu.VMEM((FT, TS, TS), BF16),
            pltpu.VMEM((2 * K, WIDE), BF16),
            pltpu.VMEM((2 * K, WIDE), BF16),
            pltpu.VMEM((K, FT * TS - WIDE), F32),
            pltpu.VMEM((K, FT * TS - WIDE), F32),
            pltpu.VMEM((K, WIDE), F32),
            pltpu.VMEM((K, WIDE), F32),
            pltpu.VMEM((K, FT * TS - WIDE), F32),
            pltpu.VMEM((K, FT * TS - WIDE), F32),
            pltpu.VMEM((2, K, 4 * K), F32),
            pltpu.VMEM((COL - 1, K, 4 * K), F32),
            pltpu.VMEM((K, 4 * K), F32),
            pltpu.VMEM((K, 4 * K), F32),
            pltpu.SemaphoreType.DMA((3,)),
            pltpu.SemaphoreType.DMA((CHUNKS,)),
            pltpu.SemaphoreType.DMA((4,)),
            pltpu.SemaphoreType.DMA((4,)),
            pltpu.SemaphoreType.DMA((COL - 1,)),
            pltpu.SemaphoreType.DMA((COL - 1,)),
            pltpu.SemaphoreType.DMA,
            pltpu.SemaphoreType.DMA,
        ],
        compiler_params=pltpu.CompilerParams(
            collective_id=0, has_side_effects=True, vmem_limit_bytes=60 * 2**20
        ),
    )(defl, diag, vals, cols, west, north)


NODES = COL - 1


def chain_kernel(got_ref, coarse_ref, pivot_ref, mult_ref):
    col = lax.axis_index("gy")
    eye = (
        lax.broadcasted_iota(jnp.int32, (K, K), 0) == lax.broadcasted_iota(jnp.int32, (K, K), 1)
    ).astype(F32)

    def eliminate(stride, held, links, solved):
        fresh = {}
        for k, inv in solved.items():
            near = links[k - stride][0]
            if k + stride in held:
                far, far_t = links[k]
                outer = exact(jnp.concatenate([near, far_t], axis=0), inv)
                to_near = exact_nt(outer, near)
                to_far = exact(outer, far)
                held[k - stride] = held[k - stride] - to_near[0:K]
                held[k + stride] = held[k + stride] - to_far[K : 2 * K]
                fresh[k - stride] = (-to_far[0:K], -to_near[K : 2 * K])
            else:
                held[k - stride] = held[k - stride] - exact_nt(exact(near, inv), near)
        return {k: held[k] for k in held if k not in solved}, fresh

    def solve(count):
        own = got_ref[COL - 1]
        self_own = own[:, 0:K]
        west_own = (own + got_ref[0])[:, K : 2 * K]
        west_own = jnp.where(col > 0, west_own, 0.0)
        coarse_ref[0, 0, 0] = self_own
        coarse_ref[0, 0, 1] = west_own
        coarse_ref[0, 0, 2] = own[:, 2 * K : 3 * K]
        held = {k: jnp.where(k < col, got_ref[k][:, 0:K], eye) for k in range(0, count, 2)}
        links = {}
        for k in range(count - 1):
            both = got_ref[k] + got_ref[k + 1]
            if k % 2:
                links[k] = (both[:, K : 2 * K], both[:, 3 * K : 4 * K])
            else:
                links[k] = (both[:, 2 * K : 3 * K],)
        odd = {k: got_ref[k][:, 0:K] for k in range(1, count, 2)}
        full, links = eliminate(1, held, links, odd)
        stride = 2
        while stride < count:
            gone = list(range(stride, count, 2 * stride))
            solved = inverses([full[k] for k in gone], 8)
            full, links = eliminate(stride, full, links, dict(zip(gone, solved, strict=True)))
            stride *= 2
        [last] = inverses([full[0]], 16)
        mult = exact(west_own, last)
        pivot_ref[0, 0] = self_own - exact_nt(mult, west_own)
        mult_ref[0, 0] = mult

    pl.when(col <= 4)(functools.partial(solve, 4))
    pl.when(jnp.logical_and(col > 4, col <= 8))(functools.partial(solve, 8))
    pl.when(col > 8)(functools.partial(solve, NODES))


def local(defl, diag, vals, cols, west, north):
    got = made_blocks(defl, diag, vals, jnp.swapaxes(cols, 2, 3), west, north)
    vmem = pl.BlockSpec(memory_space=pltpu.VMEM)
    return pl.pallas_call(
        chain_kernel,
        out_shape=(
            jax.ShapeDtypeStruct((1, 1, 3, K, K), F32),
            jax.ShapeDtypeStruct((1, 1, K, K), F32),
            jax.ShapeDtypeStruct((1, 1, K, K), F32),
        ),
        in_specs=[vmem],
        out_specs=(vmem, vmem, vmem),
        compiler_params=pltpu.CompilerParams(vmem_limit_bytes=16 * 2**20),
    )(got)


def solution(mesh):
    placed = (
        P("gx", "gy", None, None),
        P("gx", "gy", None),
        P("gx", "gy", None, None, None, None),
        P("gx", "gy", None, None),
        P("gx", "gy", None, None, None),
        P("gx", "gy", None, None, None),
    )
    return jax.shard_map(
        local,
        mesh=mesh,
        in_specs=placed,
        out_specs=(
            P("gx", "gy", None, None, None),
            P("gx", "gy", None, None),
            P("gx", "gy", None, None),
        ),
        check_vma=False,
    )
```
